32 devices in a mesh: seq: 16 (over z, y, x), chan: 2 (over core).
Axes of the slice: x: 2, y: 2, z: 4, core: 2. Of those that a mesh axis runs over, the one named last changes fastest.
Arguments:
- projected: bfloat16 [2048, 3, 4096], P('seq', None, 'chan'), may hold values from -6 to 6
- short_weight: float32 [3, 3, 4096], P(None, None, 'chan'), may hold values from -3 to 3
- filter_taps: float32 [2048, 4096], P('seq', 'chan'), may hold values from -1 to 1, as said below
- skip_gain: float32 [4096], P('chan'), may hold values from -4 to 4
- stream: bfloat16 [2048, 4096], P('seq', 'chan'), may hold values from -6 to 6
- norm_gain: float32 [4096], P('chan'), may hold values from 0.5 to 1.5
Outputs:
- mixed: bfloat16 [2048, 4096], P('seq', 'chan')
- normed: bfloat16 [2048, 4096], P('seq', 'chan')
The draws below stay inside these ranges and needn't reach their ends.
Inputs may be any that keep to these rules, and one draw needn't show every extreme that they name: `filter_taps`: taps of a causal filter.
All inputs are finite; a program needn't handle non-finite values.
Results may differ from the reference program's by a relative error of at most 0.001.
Values may be sent and summed in bfloat16 or wider, within the bound.
A program may use at most 64 MiB of HBM per device.

```python
import jax
import jax.numpy as jnp
from jax import lax

D = 4096
TOKENS = 2048


def draw_filter_taps(key, part):
    key = jax.random.fold_in(key, 7)
    key_rate = jax.random.fold_in(key, 1)
    key_noise = jax.random.fold_in(key, 2)
    longest = TOKENS / 2.3
    shortest = 40.0
    noise = jnp.clip(jax.random.normal(key_noise, (TOKENS, D), jnp.float32), -4.0, 4.0)
    span = jnp.exp(jax.random.uniform(key_rate, (D,), jnp.float32, jnp.log(shortest), jnp.log(longest)))
    amplitude = jnp.sqrt(2.0 / span)
    position = jnp.arange(TOKENS, dtype=jnp.float32)[:, None]
    taps = noise * amplitude * jnp.exp(-position / span)
    return jnp.clip(taps, -1.0, 1.0)


def block_scale(own_key, dims, shards, low, top_value):
    def one(axis_at, blocks):
        steps = jax.random.uniform(jax.random.fold_in(jax.random.fold_in(own_key, 6), axis_at), (blocks,), jnp.float32, low / len(shards), top_value / len(shards))
        return jnp.repeat(jnp.exp(steps), dims[axis_at] // blocks).reshape((-1,) + (1,) * (len(dims) - axis_at - 1))

    factor_of = one(*shards[0])
    for cut in shards[1:]:
        factor_of = factor_of * one(*cut)
    return factor_of


def centred(rng, dims, deviation, reach, split=(), kind=jnp.bfloat16):
    entries = jax.random.normal(rng, dims, jnp.float32) * deviation
    if len(split) > 0:
        entries = block_scale(rng, dims, split, -0.22, 0.18) * entries
    return jnp.clip(entries, min=-reach, max=reach).astype(kind)


def setup_inputs(seed: int = 0) -> dict:
    streams_of = jax.random.split(jax.random.key(seed), 7)
    return {
        "projected": centred(streams_of[0], (TOKENS, 3, D), 1.0, 6.0, ((0, 16), (2, 2))),
        "short_weight": centred(streams_of[1], (3, 3, D), 0.6, 3.0, ((2, 2),), jnp.float32),
        "filter_taps": draw_filter_taps(jax.random.fold_in(streams_of[6], 71), 0),
        "skip_gain": centred(streams_of[3], (D,), 1.0, 4.0, ((0, 2),), jnp.float32),
        "stream": centred(streams_of[4], (TOKENS, D), 1.0, 6.0, ((0, 16), (1, 2))),
        "norm_gain": jnp.clip(1.0 + 0.1 * jax.random.normal(streams_of[5], (D,), jnp.float32), 0.5, 1.5),
    }


def reference(projected, short_weight, filter_taps, skip_gain, stream, norm_gain):
    proj = projected.astype(jnp.float32)
    zero_rows = jnp.zeros((2, 3, D), jnp.float32)
    ext = jnp.concatenate([zero_rows, proj], axis=0)
    featured = short_weight[0] * ext[2:] + short_weight[1] * ext[1:-1] + short_weight[2] * ext[:-2]
    x_one = featured[:, 0]
    x_two = featured[:, 1]
    values = featured[:, 2]
    gated = x_two * values
    block = min(D, 256)
    nblocks = D // block
    gated_blocks = gated.T.reshape(nblocks, block, TOKENS)
    filter_blocks = filter_taps.T.reshape(nblocks, block, TOKENS)

    def convolve(pair):
        signal, taps = pair
        length = 2 * TOKENS
        spec = jnp.fft.rfft(signal, n=length, axis=1) * jnp.fft.rfft(taps, n=length, axis=1)
        return jnp.fft.irfft(spec, n=length, axis=1)[:, :TOKENS].astype(jnp.float32)
    conv = lax.map(convolve, (gated_blocks, filter_blocks)).reshape(D, TOKENS).T
    mixer = (conv + skip_gain * gated) * x_one
    mixed = mixer.astype(jnp.bfloat16)
    summed = stream.astype(jnp.float32) + mixer
    power = lax.optimization_barrier(jnp.sum(summed * summed, axis=1, keepdims=True))
    normed = (summed / jnp.sqrt(power / D + 1e-05) * norm_gain).astype(jnp.bfloat16)
    return (mixed, normed)
```

```python
import functools
import math

import jax
import jax.numpy as jnp
import ml_dtypes
import numpy as np
from jax import lax
from jax.experimental import pallas as pl
from jax.experimental.pallas import tpu as pltpu
from jax.sharding import PartitionSpec as P

D = 4096


high = lax.Precision.HIGHEST


def shifted(x, axis, by):
    count = lax.axis_size(axis)
    pairs = [(i, i + by) for i in range(count) if 0 <= i + by < count]
    return lax.ppermute(x, axis, pairs)


def tables(rows, cols, length):
    product = rows[:, None] * cols[None, :] % length
    angle = 2.0 * math.pi / length * product.astype(jnp.float32)
    return (jnp.cos(angle), jnp.sin(angle))


def local_convolve(signals, groups, rows):
    total = 2 * groups * rows
    chans = signals.shape[1]
    blocks_io = jnp.arange(groups, dtype=jnp.int32)
    freq_io = jnp.arange(2 * groups, dtype=jnp.int32)
    pos_io = jnp.arange(rows, dtype=jnp.int32)
    cos_outer, sin_outer = tables(freq_io, blocks_io, 2 * groups)
    cos_twist, sin_twist = tables(freq_io, pos_io, total)
    cos_inner, sin_inner = tables(pos_io, pos_io, rows)
    shaped = signals.reshape(2, chans, groups, rows)
    outer_re = jnp.einsum("ka,wcab->wckb", cos_outer, shaped, precision=high)
    outer_im = -jnp.einsum("ka,wcab->wckb", sin_outer, shaped, precision=high)
    turn_re = outer_re * cos_twist + outer_im * sin_twist
    turn_im = outer_im * cos_twist - outer_re * sin_twist
    spec_re = jnp.einsum("wckb,bf->wckf", turn_re, cos_inner, precision=high) + jnp.einsum(
        "wckb,bf->wckf", turn_im, sin_inner, precision=high
    )
    spec_im = jnp.einsum("wckb,bf->wckf", turn_im, cos_inner, precision=high) - jnp.einsum(
        "wckb,bf->wckf", turn_re, sin_inner, precision=high
    )
    prod_re = spec_re[0] * spec_re[1] - spec_im[0] * spec_im[1]
    prod_im = spec_re[0] * spec_im[1] + spec_im[0] * spec_re[1]
    inner_re = jnp.einsum("ckf,fb->ckb", prod_re, cos_inner, precision=high) - jnp.einsum(
        "ckf,fb->ckb", prod_im, sin_inner, precision=high
    )
    inner_im = jnp.einsum("ckf,fb->ckb", prod_im, cos_inner, precision=high) + jnp.einsum(
        "ckf,fb->ckb", prod_re, sin_inner, precision=high
    )
    back_re = inner_re * cos_twist - inner_im * sin_twist
    back_im = inner_im * cos_twist + inner_re * sin_twist
    cos_final, sin_final = tables(blocks_io, freq_io, 2 * groups)
    result = jnp.einsum("ak,ckb->cab", cos_final, back_re, precision=high) - jnp.einsum(
        "ak,ckb->cab", sin_final, back_im, precision=high
    )
    return (result / total).reshape(chans, groups * rows)


def shards(projected, short_weight, filter_taps, skip_gain, stream, norm_gain):
    rows = projected.shape[0]
    groups = lax.axis_size("seq")
    previous = shifted(projected[rows - 2 :], "seq", 1)
    ext = jnp.concatenate([previous, projected], axis=0).astype(jnp.float32)
    featured = short_weight[0] * ext[2:] + short_weight[1] * ext[1:-1] + short_weight[2] * ext[:-2]
    x_one = featured[:, 0]
    gated = featured[:, 1] * featured[:, 2]
    whole = lax.all_to_all(
        jnp.stack([gated, filter_taps]), "seq", split_axis=2, concat_axis=1, tiled=True
    )
    signals = jnp.transpose(whole, (0, 2, 1))
    convolved = local_convolve(signals, groups, rows)
    conv = lax.all_to_all(convolved.T, "seq", split_axis=0, concat_axis=1, tiled=True)
    mixer = (conv + skip_gain * gated) * x_one
    mixed = mixer.astype(jnp.bfloat16)
    summed = stream.astype(jnp.float32) + mixer
    power = lax.psum(jnp.sum(summed * summed, axis=1), "chan")
    normed = (summed / jnp.sqrt(power[:, None] / D + 1e-05) * norm_gain).astype(jnp.bfloat16)
    return (mixed, normed)


MESH = pl.DeviceIdType.MESH
POWER = 16
TOP = 2.0**7.75


def encode(x):
    most = jnp.maximum(jnp.max(jnp.abs(x), axis=0, keepdims=True), 1e-30)
    r = x * (TOP / most)
    p = r * r
    p = p * p
    p = p * p
    p = p * p
    return jnp.where(r < 0.0, -p, p).astype(jnp.bfloat16), most * (1.0 / TOP)


def decode(code, scale):
    y = code.astype(jnp.float32)
    mag = jnp.abs(y)
    root = jnp.exp(jnp.log(jnp.maximum(mag, 1e-38)) * (1.0 / POWER)) * scale
    root = jnp.where(mag > 0.0, root, 0.0)
    return jnp.where(y < 0.0, -root, root)


def split3(x):
    hi = x.astype(jnp.bfloat16)
    lo = (x - hi.astype(jnp.float32)).astype(jnp.bfloat16)
    return jnp.concatenate([hi, lo, hi], axis=0)


def dot(a, b):
    return jnp.dot(a, b, preferred_element_type=jnp.float32)


def wide(mat):
    hi = mat.astype(ml_dtypes.bfloat16)
    lo = (mat - hi.astype(np.float64)).astype(ml_dtypes.bfloat16)
    return np.concatenate([hi, hi, lo], axis=1)


def constants(groups, rows, fine):
    total = 2 * groups * rows
    ks = groups + 2
    k = np.arange(ks)
    a = np.arange(groups)
    b = np.arange(rows)
    live = (k <= groups).astype(np.float64)
    angle = 2.0 * np.pi * (k[:, None] * a[None, :] % (2 * groups)) / (2 * groups)
    eye = np.eye(fine)
    fwd = np.stack([np.cos(angle), -np.sin(angle)], axis=1) * live[:, None, None]
    outer = np.einsum("kra,xy->krxay", fwd, eye).reshape(ks * 2 * fine, groups * fine)
    weight = np.where((k == 0) | (k == groups), 1.0, 2.0) * live / total
    back = np.einsum("kra,xy->axkry", fwd * weight[:, None, None], eye)
    back = back.reshape(groups * fine, ks * 2 * fine)
    inner = 2.0 * np.pi * (b[:, None] * b[None, :] % rows) / rows
    c, s = np.cos(inner), np.sin(inner)
    mat = np.block([[c, s], [-s, c]])
    turn = 2.0 * np.pi * (k[:, None] * b[None, :] % total) / total
    spread = np.stack([np.cos(turn), np.sin(turn)], axis=1)[..., None]
    spread = np.broadcast_to(spread, (ks, 2, rows, 128)).astype(np.float32)
    return wide(outer), wide(mat), wide(mat.T), wide(back), spread


def greet(axis, n, me):
    barrier = pltpu.get_barrier_semaphore()
    for o in range(1, n):
        pl.semaphore_signal(
            barrier, inc=1, device_id={axis: lax.rem(me + o, n)}, device_id_type=MESH
        )
    return barrier


def fan_out(n, me, pairs):
    copies = []
    for o in range(1, n):
        to = lax.rem(me + o, n)
        for src, dst, send, recv in pairs:
            copy = pltpu.make_async_remote_copy(
                src_ref=src.at[to],
                dst_ref=dst.at[me],
                send_sem=send.at[o],
                recv_sem=recv.at[o],
                device_id={"seq": to},
                device_id_type=MESH,
            )
            copy.start()
            copies.append(copy)
    return copies


def exchange_kernel(
    n, x_ref, w_ref, taps_ref, hcode, hscale, gcode, gscale, gated_ref, one_ref,
    hsend, hsscale, gsend, gsscale, tail, halo, sems,
):
    me = lax.axis_index("seq")
    rows = x_ref.shape[1]
    barrier = greet("seq", n, me)
    for j in range(3):
        last = x_ref[j, rows - 16 :, :].astype(jnp.float32)
        tail[2 * j : 2 * j + 2, :] = last[14:16, :]

    def pack_taps(d, carry):
        cols = pl.ds(pl.multiple_of(d * 128, 128), 128)
        code, scale = encode(taps_ref[:, cols])
        hsend[d] = code
        hsscale[d] = scale
        return carry

    lax.fori_loop(0, n, pack_taps, 0)
    pl.semaphore_wait(barrier, n - 1)
    after = pltpu.make_async_remote_copy(
        src_ref=tail,
        dst_ref=halo,
        send_sem=sems.at[8, 0],
        recv_sem=sems.at[8, 1],
        device_id={"seq": lax.rem(me + 1, n)},
        device_id_type=MESH,
    )
    after.start()
    copies = fan_out(
        n, me,
        [(hsend, hcode, sems.at[0], sems.at[1]), (hsscale, hscale, sems.at[2], sems.at[3])],
    )
    hcode[me] = hsend[me]
    hscale[me] = hsscale[me]
    after.wait()
    first = jnp.where(me > 0, 1.0, 0.0).astype(jnp.float32)

    def pack_gated(d, carry):
        cols = pl.ds(pl.multiple_of(d * 128, 128), 128)
        prev = halo[:, cols] * first
        w = w_ref[:, cols]
        feats = []
        for j in range(3):
            x = x_ref[j, :, cols].astype(jnp.float32)
            ext = jnp.concatenate([prev[2 * j : 2 * j + 2], x], axis=0)
            feats.append(
                w[j : j + 1] * x + w[3 + j : 4 + j] * ext[1 : rows + 1] + w[6 + j : 7 + j] * ext[:rows]
            )
        gated = feats[1] * feats[2]
        one_ref[:, cols] = feats[0]
        gated_ref[:, cols] = gated
        code, scale = encode(gated)
        gsend[d] = code
        gsscale[d] = scale
        return carry

    lax.fori_loop(0, n, pack_gated, 0)
    copies += fan_out(
        n, me,
        [(gsend, gcode, sems.at[4], sems.at[5]), (gsscale, gscale, sems.at[6], sems.at[7])],
    )
    gcode[me] = gsend[me]
    gscale[me] = gsscale[me]
    for copy in copies:
        copy.wait()


def outer_forward(n, rows, code, scale, outer, x, y):
    def unpack(a, carry):
        x[a] = decode(code[a], scale[a])
        return carry

    lax.fori_loop(0, n, unpack, 0)
    ks = n + 2

    def step(j, carry):
        parts = []
        for half in range(2):
            at = pl.ds(pl.multiple_of(j * 32 + 16 * half, 16), 16)
            parts.append(x[:, at, :].reshape(n * 16, 128))
        u = dot(outer[...], split3(jnp.concatenate(parts, axis=1)))
        for half in range(2):
            at = pl.ds(pl.multiple_of(j * 32 + 16 * half, 16), 16)
            y[:, :, at, :] = u[:, 128 * half : 128 * half + 128].reshape(ks, 2, 16, 128)
        return carry

    lax.fori_loop(0, rows // 32, step, 0)


def inner_forward(pair, rows, inner, turn, y):
    parts = []
    for half in range(2):
        k = 2 * pair + half
        re, im, c, s = y[k, 0], y[k, 1], turn[k, 0], turn[k, 1]
        parts.append(jnp.concatenate([re * c + im * s, im * c - re * s], axis=0))
    return dot(inner[...], split3(jnp.concatenate(parts, axis=1)))


def taps_spectrum(n, rows, hcode, hscale, outer, inner, turn, x, y, z):
    outer_forward(n, rows, hcode, hscale, outer, x, y)

    def step(pair, carry):
        z[pair] = inner_forward(pair, rows, inner, turn, y)
        return carry

    lax.fori_loop(0, (n + 2) // 2, step, 0)


def convolve(n, rows, gcode, gscale, outer, inner, inner_back, back, turn, x, y, z, code, scale):
    outer_forward(n, rows, gcode, gscale, outer, x, y)

    def step(pair, carry):
        g = inner_forward(pair, rows, inner, turn, y)
        h = z[pair]
        gr, gi, hr, hi = g[:rows], g[rows:], h[:rows], h[rows:]
        prod = jnp.concatenate([gr * hr - gi * hi, gr * hi + gi * hr], axis=0)
        v = dot(inner_back[...], split3(prod))
        for half in range(2):
            k = 2 * pair + half
            lanes = slice(128 * half, 128 * half + 128)
            re, im, c, s = v[:rows, lanes], v[rows:, lanes], turn[k, 0], turn[k, 1]
            y[k, 0] = re * c - im * s
            y[k, 1] = im * c + re * s
        return carry

    lax.fori_loop(0, (n + 2) // 2, step, 0)

    def last(j, carry):
        parts = []
        for half in range(2):
            at = pl.ds(pl.multiple_of(j * 32 + 16 * half, 16), 16)
            parts.append(y[:, :, at, :].reshape((n + 2) * 32, 128))
        u = dot(back[...], split3(jnp.concatenate(parts, axis=1)))
        for half in range(2):
            at = pl.ds(pl.multiple_of(j * 32 + 16 * half, 16), 16)
            x[:, at, :] = u[:, 128 * half : 128 * half + 128].reshape(n, 16, 128)
        return carry

    lax.fori_loop(0, rows // 32, last, 0)

    def pack(a, carry):
        code[a], scale[a] = encode(x[a])
        return carry

    lax.fori_loop(0, n, pack, 0)


def convolve_kernel(
    n, rows, hcode, hscale, gcode, gscale, outer, inner, inner_back, back, turn,
    code, scale, x, y, z,
):
    taps_spectrum(n, rows, hcode, hscale, outer, inner, turn, x, y, z)
    convolve(n, rows, gcode, gscale, outer, inner, inner_back, back, turn, x, y, z, code, scale)


def finish_kernel(
    n, code, scale, gated_ref, one_ref, stream_ref, skip_ref, gain_ref, mixed_ref, normed_ref,
    ccode, cscale, summed, mine, other, sems,
):
    me = lax.axis_index("seq")
    core = lax.axis_index("chan")
    barrier = greet("seq", n, me)
    pl.semaphore_signal(barrier, inc=1, device_id={"chan": 1 - core}, device_id_type=MESH)
    pl.semaphore_wait(barrier, n)
    copies = fan_out(
        n, me,
        [(code, ccode, sems.at[0], sems.at[1]), (scale, cscale, sems.at[2], sems.at[3])],
    )
    ccode[me] = code[me]
    cscale[me] = scale[me]
    for copy in copies:
        copy.wait()
    mine[...] = jnp.zeros_like(mine)

    def mix(d, carry):
        cols = pl.ds(pl.multiple_of(d * 128, 128), 128)
        conv = decode(ccode[d], cscale[d])
        mixer = (conv + skip_ref[:, cols] * gated_ref[:, cols]) * one_ref[:, cols]
        mixed_ref[:, cols] = mixer.astype(jnp.bfloat16)
        both = stream_ref[:, cols].astype(jnp.float32) + mixer
        summed[:, cols] = both
        mine[...] += both * both
        return carry

    lax.fori_loop(0, n, mix, 0)
    swap = pltpu.make_async_remote_copy(
        src_ref=mine,
        dst_ref=other,
        send_sem=sems.at[4, 0],
        recv_sem=sems.at[4, 1],
        device_id={"chan": 1 - core},
        device_id_type=MESH,
    )
    swap.start()
    swap.wait()
    power = jnp.sum(mine[...] + other[...], axis=1, keepdims=True)
    factor = 1.0 / jnp.sqrt(power / D + 1e-05)

    def norm(d, carry):
        cols = pl.ds(pl.multiple_of(d * 128, 128), 128)
        normed_ref[:, cols] = (summed[:, cols] * factor * gain_ref[:, cols]).astype(jnp.bfloat16)
        return carry

    lax.fori_loop(0, n, norm, 0)


def fast(n, projected, short_weight, filter_taps, skip_gain, stream, norm_gain):
    rows, _, chans = projected.shape
    f32, bf16 = jnp.float32, jnp.bfloat16
    shape = jax.ShapeDtypeStruct
    vmem = pl.BlockSpec(memory_space=pltpu.VMEM)
    codes, scales = (n, rows, 128), (n, 1, 128)
    streams = jnp.transpose(projected, (1, 0, 2))
    hcode, hscale, gcode, gscale, gated, one = pl.pallas_call(
        functools.partial(exchange_kernel, n),
        out_shape=[
            shape(codes, bf16), shape(scales, f32), shape(codes, bf16), shape(scales, f32),
            shape((rows, chans), f32), shape((rows, chans), f32),
        ],
        in_specs=[vmem] * 3,
        out_specs=[vmem] * 6,
        scratch_shapes=[
            pltpu.VMEM(codes, bf16), pltpu.VMEM(scales, f32),
            pltpu.VMEM(codes, bf16), pltpu.VMEM(scales, f32),
            pltpu.VMEM((8, chans), f32), pltpu.VMEM((8, chans), f32),
            pltpu.SemaphoreType.DMA((9, n)),
        ],
        compiler_params=pltpu.CompilerParams(
            collective_id=0, has_side_effects=True, vmem_limit_bytes=40 * 2**20
        ),
        name="exchange",
    )(streams, short_weight.reshape(9, chans), filter_taps)
    outer, inner, inner_back, back, turn = constants(n, rows, 16)
    ks = n + 2
    code, scale = pl.pallas_call(
        functools.partial(convolve_kernel, n, rows),
        out_shape=[shape(codes, bf16), shape(scales, f32)],
        in_specs=[vmem] * 9,
        out_specs=[vmem] * 2,
        scratch_shapes=[
            pltpu.VMEM(codes, f32),
            pltpu.VMEM((ks, 2, rows, 128), f32),
            pltpu.VMEM((ks // 2, 2 * rows, 256), f32),
        ],
        compiler_params=pltpu.CompilerParams(vmem_limit_bytes=40 * 2**20),
        name="convolve",
    )(hcode, hscale, gcode, gscale, outer, inner, inner_back, back, turn)
    return pl.pallas_call(
        functools.partial(finish_kernel, n),
        out_shape=[shape((rows, chans), bf16)] * 2,
        in_specs=[vmem] * 7,
        out_specs=[vmem] * 2,
        scratch_shapes=[
            pltpu.VMEM(codes, bf16), pltpu.VMEM(scales, f32),
            pltpu.VMEM((rows, chans), f32),
            pltpu.VMEM((rows, 128), f32), pltpu.VMEM((rows, 128), f32),
            pltpu.SemaphoreType.DMA((5, n)),
        ],
        compiler_params=pltpu.CompilerParams(
            collective_id=1, has_side_effects=True, vmem_limit_bytes=40 * 2**20
        ),
        name="finish",
    )(code, scale, gated, one, stream, skip_gain.reshape(1, chans), norm_gain.reshape(1, chans))


def solution(mesh):
    n, cores = mesh.shape["seq"], mesh.shape["chan"]

    def local(*args):
        rows, _, chans = args[0].shape
        if cores == 2 and chans == 128 * n and rows == 128 and n % 2 == 0:
            return tuple(fast(n, *args))
        return shards(*args)

    in_specs = (
        P("seq", None, "chan"),
        P(None, None, "chan"),
        P("seq", "chan"),
        P("chan"),
        P("seq", "chan"),
        P("chan"),
    )
    out_specs = (P("seq", "chan"), P("seq", "chan"))
    return jax.shard_map(local, mesh=mesh, in_specs=in_specs, out_specs=out_specs, check_vma=False)
```

```python
import functools
import math

import jax
import jax.numpy as jnp
import ml_dtypes
import numpy as np
from jax import lax
from jax.experimental import pallas as pl
from jax.experimental.pallas import tpu as pltpu
from jax.sharding import PartitionSpec as P

D = 4096


high = lax.Precision.HIGHEST


def shifted(x, axis, by):
    count = lax.axis_size(axis)
    pairs = [(i, i + by) for i in range(count) if 0 <= i + by < count]
    return lax.ppermute(x, axis, pairs)


def tables(rows, cols, length):
    product = rows[:, None] * cols[None, :] % length
    angle = 2.0 * math.pi / length * product.astype(jnp.float32)
    return (jnp.cos(angle), jnp.sin(angle))


def local_convolve(signals, groups, rows):
    total = 2 * groups * rows
    chans = signals.shape[1]
    blocks_io = jnp.arange(groups, dtype=jnp.int32)
    freq_io = jnp.arange(2 * groups, dtype=jnp.int32)
    pos_io = jnp.arange(rows, dtype=jnp.int32)
    cos_outer, sin_outer = tables(freq_io, blocks_io, 2 * groups)
    cos_twist, sin_twist = tables(freq_io, pos_io, total)
    cos_inner, sin_inner = tables(pos_io, pos_io, rows)
    shaped = signals.reshape(2, chans, groups, rows)
    outer_re = jnp.einsum("ka,wcab->wckb", cos_outer, shaped, precision=high)
    outer_im = -jnp.einsum("ka,wcab->wckb", sin_outer, shaped, precision=high)
    turn_re = outer_re * cos_twist + outer_im * sin_twist
    turn_im = outer_im * cos_twist - outer_re * sin_twist
    spec_re = jnp.einsum("wckb,bf->wckf", turn_re, cos_inner, precision=high) + jnp.einsum(
        "wckb,bf->wckf", turn_im, sin_inner, precision=high
    )
    spec_im = jnp.einsum("wckb,bf->wckf", turn_im, cos_inner, precision=high) - jnp.einsum(
        "wckb,bf->wckf", turn_re, sin_inner, precision=high
    )
    prod_re = spec_re[0] * spec_re[1] - spec_im[0] * spec_im[1]
    prod_im = spec_re[0] * spec_im[1] + spec_im[0] * spec_re[1]
    inner_re = jnp.einsum("ckf,fb->ckb", prod_re, cos_inner, precision=high) - jnp.einsum(
        "ckf,fb->ckb", prod_im, sin_inner, precision=high
    )
    inner_im = jnp.einsum("ckf,fb->ckb", prod_im, cos_inner, precision=high) + jnp.einsum(
        "ckf,fb->ckb", prod_re, sin_inner, precision=high
    )
    back_re = inner_re * cos_twist - inner_im * sin_twist
    back_im = inner_im * cos_twist + inner_re * sin_twist
    cos_final, sin_final = tables(blocks_io, freq_io, 2 * groups)
    result = jnp.einsum("ak,ckb->cab", cos_final, back_re, precision=high) - jnp.einsum(
        "ak,ckb->cab", sin_final, back_im, precision=high
    )
    return (result / total).reshape(chans, groups * rows)


def shards(projected, short_weight, filter_taps, skip_gain, stream, norm_gain):
    rows = projected.shape[0]
    groups = lax.axis_size("seq")
    previous = shifted(projected[rows - 2 :], "seq", 1)
    ext = jnp.concatenate([previous, projected], axis=0).astype(jnp.float32)
    featured = short_weight[0] * ext[2:] + short_weight[1] * ext[1:-1] + short_weight[2] * ext[:-2]
    x_one = featured[:, 0]
    gated = featured[:, 1] * featured[:, 2]
    whole = lax.all_to_all(
        jnp.stack([gated, filter_taps]), "seq", split_axis=2, concat_axis=1, tiled=True
    )
    signals = jnp.transpose(whole, (0, 2, 1))
    convolved = local_convolve(signals, groups, rows)
    conv = lax.all_to_all(convolved.T, "seq", split_axis=0, concat_axis=1, tiled=True)
    mixer = (conv + skip_gain * gated) * x_one
    mixed = mixer.astype(jnp.bfloat16)
    summed = stream.astype(jnp.float32) + mixer
    power = lax.psum(jnp.sum(summed * summed, axis=1), "chan")
    normed = (summed / jnp.sqrt(power[:, None] / D + 1e-05) * norm_gain).astype(jnp.bfloat16)
    return (mixed, normed)


MESH = pl.DeviceIdType.MESH
POWER = 16
TOP = 2.0**7.75


def encode(x):
    most = jnp.maximum(jnp.max(jnp.abs(x), axis=0, keepdims=True), 1e-30)
    r = x * (TOP / most)
    p = r * r
    p = p * p
    p = p * p
    p = p * p
    return jnp.where(r < 0.0, -p, p).astype(jnp.bfloat16), most * (1.0 / TOP)


def decode(code, scale):
    y = code.astype(jnp.float32)
    mag = jnp.abs(y)
    root = jnp.exp(jnp.log(jnp.maximum(mag, 1e-38)) * (1.0 / POWER)) * scale
    root = jnp.where(mag > 0.0, root, 0.0)
    return jnp.where(y < 0.0, -root, root)


def split3(x):
    hi = x.astype(jnp.bfloat16)
    lo = (x - hi.astype(jnp.float32)).astype(jnp.bfloat16)
    return jnp.concatenate([hi, lo, hi], axis=0)


def dot(a, b):
    return jnp.dot(a, b, preferred_element_type=jnp.float32)


def wide(mat):
    hi = mat.astype(ml_dtypes.bfloat16)
    lo = (mat - hi.astype(np.float64)).astype(ml_dtypes.bfloat16)
    return np.concatenate([hi, hi, lo], axis=1)


def constants(groups, rows, fine):
    total = 2 * groups * rows
    ks = groups + 2
    k = np.arange(ks)
    a = np.arange(groups)
    b = np.arange(rows)
    live = (k <= groups).astype(np.float64)
    angle = 2.0 * np.pi * (k[:, None] * a[None, :] % (2 * groups)) / (2 * groups)
    eye = np.eye(fine)
    fwd = np.stack([np.cos(angle), -np.sin(angle)], axis=1) * live[:, None, None]
    outer = np.einsum("kra,xy->krxay", fwd, eye).reshape(ks * 2 * fine, groups * fine)
    weight = np.where((k == 0) | (k == groups), 1.0, 2.0) * live / total
    back = np.einsum("kra,xy->axkry", fwd * weight[:, None, None], eye)
    back = back.reshape(groups * fine, ks * 2 * fine)
    inner = 2.0 * np.pi * (b[:, None] * b[None, :] % rows) / rows
    c, s = np.cos(inner), np.sin(inner)
    mat = np.block([[c, s], [-s, c]])
    turn = 2.0 * np.pi * (k[:, None] * b[None, :] % total) / total
    spread = np.stack([np.cos(turn), np.sin(turn)], axis=1)[..., None]
    spread = np.broadcast_to(spread, (ks, 2, rows, 128)).astype(np.float32)
    return wide(outer), wide(mat), wide(mat.T), wide(back), spread


def outer_forward(n, rows, outer, x, y):
    ks = n + 2

    def step(j, carry):
        parts = []
        for half in range(2):
            at = pl.ds(pl.multiple_of(j * 32 + 16 * half, 16), 16)
            parts.append(x[:, at, :].reshape(n * 16, 128))
        u = dot(outer[...], split3(jnp.concatenate(parts, axis=1)))
        for half in range(2):
            at = pl.ds(pl.multiple_of(j * 32 + 16 * half, 16), 16)
            y[:, :, at, :] = u[:, 128 * half : 128 * half + 128].reshape(ks, 2, 16, 128)
        return carry

    lax.fori_loop(0, rows // 32, step, 0)


def inner_forward(pair, rows, inner, turn, y):
    parts = []
    for half in range(2):
        k = 2 * pair + half
        re, im, c, s = y[k, 0], y[k, 1], turn[k, 0], turn[k, 1]
        parts.append(jnp.concatenate([re * c + im * s, im * c - re * s], axis=0))
    return dot(inner[...], split3(jnp.concatenate(parts, axis=1)))


def kernel(
    n, x_hbm, w_hbm, taps_hbm, skip_hbm, stream_hbm, gain_hbm, outer_hbm, inner_hbm, inner_back_hbm,
    back_hbm, turn_hbm, mixed_ref, normed_ref,
    x_ref, w_ref, taps_ref, skip_ref, stream_ref, gain_ref, outer, inner, inner_back, back, turn,
    gated_ref, one_ref, tail, halo, hsend, hsscale, hcode, hscale, gsend, gsscale, gcode, gscale,
    csend, csscale, ccode, cscale, x, y, z, summed, mine, other, sems, edge_sems, local_sems,
):
    me = lax.axis_index("seq")
    core = lax.axis_index("chan")
    rows = x_ref.shape[1]
    part = rows // 2
    barrier = pltpu.get_barrier_semaphore()

    def greet(o, carry):
        pl.semaphore_signal(
            barrier, inc=1, device_id={"seq": lax.rem(me + o, n)}, device_id_type=MESH
        )
        return carry

    lax.fori_loop(1, n, greet, 0)
    pl.semaphore_signal(barrier, inc=1, device_id={"chan": 1 - core}, device_id_type=MESH)

    moves = [(x_hbm, x_ref), (taps_hbm, taps_ref), (w_hbm, w_ref), (outer_hbm, outer),
             (turn_hbm, turn), (inner_hbm, inner), (inner_back_hbm, inner_back), (back_hbm, back),
             (stream_hbm, stream_ref), (skip_hbm, skip_ref), (gain_hbm, gain_ref)]
    loads = []
    for i, (src, dst) in enumerate(moves):
        load = pltpu.make_async_copy(src, dst, local_sems.at[i])
        load.start()
        loads.append(load)

    def lanes(d):
        return pl.ds(pl.multiple_of(d * 128, 128), 128)

    def link(kind, o, src, dst):
        return pltpu.make_async_remote_copy(
            src_ref=src,
            dst_ref=dst,
            send_sem=sems.at[2 * kind, o],
            recv_sem=sems.at[2 * kind + 1, o],
            device_id={"seq": lax.rem(me + o, n)},
            device_id_type=MESH,
        )

    def taps_links(o):
        to = lax.rem(me + o, n)
        return (link(0, o, hsend.at[to], hcode.at[me]), link(1, o, hsscale.at[to], hscale.at[me]))

    def gated_links(o):
        to = lax.rem(me + o, n)
        return (link(2, o, gsend.at[to], gcode.at[me]), link(3, o, gsscale.at[to], gscale.at[me]))

    def conv_links(p, o):
        to = lax.rem(me + o, n)
        at = pl.ds(p * part, part)
        return (
            link(4 + 2 * p, o, csend.at[to, at], ccode.at[me, at]),
            link(5 + 2 * p, o, csscale.at[p, to], cscale.at[p, me]),
        )

    loads[0].wait()
    for j in range(3):
        last = x_ref[j, rows - 16 :, :].astype(jnp.float32)
        tail[2 * j : 2 * j + 2, :] = last[14:16, :]
    loads[1].wait()
    pl.semaphore_wait(barrier, n)
    after = pltpu.make_async_remote_copy(
        src_ref=tail,
        dst_ref=halo,
        send_sem=edge_sems.at[0],
        recv_sem=edge_sems.at[1],
        device_id={"seq": lax.rem(me + 1, n)},
        device_id_type=MESH,
    )
    after.start()

    def send_taps(o, carry):
        to = lax.rem(me + o, n)
        hsend[to], hsscale[to] = encode(taps_ref[:, lanes(to)])
        for copy in taps_links(o):
            copy.start()
        return carry

    lax.fori_loop(1, n, send_taps, 0)
    x[me] = taps_ref[:, lanes(me)]
    loads[2].wait()
    after.wait()
    first = jnp.where(me > 0, 1.0, 0.0).astype(jnp.float32)

    def feature(d):
        cols = lanes(d)
        prev = halo[:, cols] * first
        feats = []
        for j in range(3):
            now = x_ref[j, :, cols].astype(jnp.float32)
            ext = jnp.concatenate([prev[2 * j : 2 * j + 2], now], axis=0)
            feats.append(
                w_ref[0, j : j + 1, cols] * now
                + w_ref[1, j : j + 1, cols] * ext[1 : rows + 1]
                + w_ref[2, j : j + 1, cols] * ext[:rows]
            )
        gated = feats[1] * feats[2]
        one_ref[:, cols] = feats[0]
        gated_ref[:, cols] = gated
        return gated

    def send_gated(o, carry):
        to = lax.rem(me + o, n)
        gsend[to], gsscale[to] = encode(feature(to))
        for copy in gated_links(o):
            copy.start()
        return carry

    lax.fori_loop(1, n, send_gated, 0)
    feature(me)

    def take_taps(o, carry):
        source = lax.rem(me - o + n, n)
        for copy in taps_links(o):
            copy.wait()
        x[source] = decode(hcode[source], hscale[source])
        return carry

    lax.fori_loop(1, n, take_taps, 0)
    for load in loads[3:8]:
        load.wait()
    outer_forward(n, rows, outer, x, y)

    def spectrum(pair, carry):
        z[pair] = inner_forward(pair, rows, inner, turn, y)
        return carry

    lax.fori_loop(0, (n + 2) // 2, spectrum, 0)
    x[me] = gated_ref[:, lanes(me)]

    def take_gated(o, carry):
        source = lax.rem(me - o + n, n)
        for copy in gated_links(o):
            copy.wait()
        x[source] = decode(gcode[source], gscale[source])
        return carry

    lax.fori_loop(1, n, take_gated, 0)
    outer_forward(n, rows, outer, x, y)

    def multiply(pair, carry):
        g = inner_forward(pair, rows, inner, turn, y)
        h = z[pair]
        gr, gi, hr, hi = g[:rows], g[rows:], h[:rows], h[rows:]
        prod = jnp.concatenate([gr * hr - gi * hi, gr * hi + gi * hr], axis=0)
        v = dot(inner_back[...], split3(prod))
        for half in range(2):
            k = 2 * pair + half
            side = slice(128 * half, 128 * half + 128)
            re, im, c, s = v[:rows, side], v[rows:, side], turn[k, 0], turn[k, 1]
            y[k, 0] = re * c - im * s
            y[k, 1] = im * c + re * s
        return carry

    lax.fori_loop(0, (n + 2) // 2, multiply, 0)

    def blocks(j, carry):
        parts = []
        for half in range(2):
            at = pl.ds(pl.multiple_of(j * 32 + 16 * half, 16), 16)
            parts.append(y[:, :, at, :].reshape((n + 2) * 32, 128))
        u = dot(back[...], split3(jnp.concatenate(parts, axis=1)))
        for half in range(2):
            at = pl.ds(pl.multiple_of(j * 32 + 16 * half, 16), 16)
            x[:, at, :] = u[:, 128 * half : 128 * half + 128].reshape(n, 16, 128)
        return carry

    for p in range(2):
        lax.fori_loop(p * part // 32, (p + 1) * part // 32, blocks, 0)

        def send_conv(o, carry, p=p):
            to = lax.rem(me + o, n)
            at = pl.ds(p * part, part)
            csend[to, at, :], csscale[p, to] = encode(x[to, at, :])
            for copy in conv_links(p, o):
                copy.start()
            return carry

        lax.fori_loop(1, n, send_conv, 0)

    for load in loads[8:]:
        load.wait()
    mine[...] = jnp.zeros_like(mine)

    def mix(p, d, conv):
        at, cols = pl.ds(p * part, part), lanes(d)
        mixer = (conv + skip_ref[:, cols] * gated_ref[at, cols]) * one_ref[at, cols]
        mixed_ref[at, cols] = mixer.astype(jnp.bfloat16)
        both = stream_ref[at, cols].astype(jnp.float32) + mixer
        summed[at, cols] = both
        mine[at, :] += both * both

    for p in range(2):
        mix(p, me, x[me, pl.ds(p * part, part), :])

        def take_conv(o, carry, p=p):
            source = lax.rem(me - o + n, n)
            for copy in conv_links(p, o):
                copy.wait()
            mix(p, source, decode(ccode[source, pl.ds(p * part, part), :], cscale[p, source]))
            return carry

        lax.fori_loop(1, n, take_conv, 0)

    swap = pltpu.make_async_remote_copy(
        src_ref=mine,
        dst_ref=other,
        send_sem=edge_sems.at[2],
        recv_sem=edge_sems.at[3],
        device_id={"chan": 1 - core},
        device_id_type=MESH,
    )
    swap.start()
    swap.wait()
    power = jnp.sum(mine[...] + other[...], axis=1, keepdims=True)
    factor = 1.0 / jnp.sqrt(power / D + 1e-05)

    def norm(d, carry):
        cols = lanes(d)
        normed_ref[:, cols] = (summed[:, cols] * factor * gain_ref[:, cols]).astype(jnp.bfloat16)
        return carry

    lax.fori_loop(0, n, norm, 0)


def fast(n, projected, short_weight, filter_taps, skip_gain, stream, norm_gain):
    rows, _, chans = projected.shape
    f32, bf16 = jnp.float32, jnp.bfloat16
    codes, scales, ks = (n, rows, 128), (n, 1, 128), n + 2
    operands = [
        jnp.transpose(projected, (1, 0, 2)), short_weight, filter_taps,
        skip_gain.reshape(1, chans), stream, norm_gain.reshape(1, chans),
    ] + [jnp.asarray(table) for table in constants(n, rows, 16)]
    pair = [pltpu.VMEM(codes, bf16), pltpu.VMEM(scales, f32)]
    return pl.pallas_call(
        functools.partial(kernel, n),
        out_shape=[jax.ShapeDtypeStruct((rows, chans), bf16)] * 2,
        in_specs=[pl.BlockSpec(memory_space=pl.ANY)] * len(operands),
        out_specs=[pl.BlockSpec(memory_space=pltpu.VMEM)] * 2,
        scratch_shapes=[pltpu.VMEM(array.shape, array.dtype) for array in operands]
        + [pltpu.VMEM((rows, chans), f32)] * 2
        + [pltpu.VMEM((8, chans), f32)] * 2
        + pair * 4
        + [pltpu.VMEM(codes, bf16), pltpu.VMEM((2,) + scales, f32)] * 2
        + [
            pltpu.VMEM(codes, f32),
            pltpu.VMEM((ks, 2, rows, 128), f32),
            pltpu.VMEM((ks // 2, 2 * rows, 256), f32),
            pltpu.VMEM((rows, chans), f32),
            pltpu.VMEM((rows, 128), f32),
            pltpu.VMEM((rows, 128), f32),
            pltpu.SemaphoreType.DMA((16, n)),
            pltpu.SemaphoreType.DMA((4,)),
            pltpu.SemaphoreType.DMA((len(operands),)),
        ],
        compiler_params=pltpu.CompilerParams(
            collective_id=0, has_side_effects=True, vmem_limit_bytes=56 * 2**20
        ),
        name="mixer",
    )(*operands)


def solution(mesh):
    n, cores = mesh.shape["seq"], mesh.shape["chan"]

    def local(*args):
        rows, _, chans = args[0].shape
        if cores == 2 and chans == 128 * n and rows == 128 and n % 2 == 0:
            return tuple(fast(n, *args))
        return shards(*args)

    in_specs = (
        P("seq", None, "chan"),
        P(None, None, "chan"),
        P("seq", "chan"),
        P("chan"),
        P("seq", "chan"),
        P("chan"),
    )
    out_specs = (P("seq", "chan"), P("seq", "chan"))
    return jax.shard_map(local, mesh=mesh, in_specs=in_specs, out_specs=out_specs, check_vma=False)
```

```python
import functools
import math

import jax
import jax.numpy as jnp
import ml_dtypes
import numpy as np
from jax import lax
from jax.experimental import pallas as pl
from jax.experimental.pallas import tpu as pltpu
from jax.sharding import PartitionSpec as P

D = 4096


high = lax.Precision.HIGHEST


def shifted(x, axis, by):
    count = lax.axis_size(axis)
    pairs = [(i, i + by) for i in range(count) if 0 <= i + by < count]
    return lax.ppermute(x, axis, pairs)


def tables(rows, cols, length):
    product = rows[:, None] * cols[None, :] % length
    angle = 2.0 * math.pi / length * product.astype(jnp.float32)
    return (jnp.cos(angle), jnp.sin(angle))


def local_convolve(signals, groups, rows):
    total = 2 * groups * rows
    chans = signals.shape[1]
    blocks_io = jnp.arange(groups, dtype=jnp.int32)
    freq_io = jnp.arange(2 * groups, dtype=jnp.int32)
    pos_io = jnp.arange(rows, dtype=jnp.int32)
    cos_outer, sin_outer = tables(freq_io, blocks_io, 2 * groups)
    cos_twist, sin_twist = tables(freq_io, pos_io, total)
    cos_inner, sin_inner = tables(pos_io, pos_io, rows)
    shaped = signals.reshape(2, chans, groups, rows)
    outer_re = jnp.einsum("ka,wcab->wckb", cos_outer, shaped, precision=high)
    outer_im = -jnp.einsum("ka,wcab->wckb", sin_outer, shaped, precision=high)
    turn_re = outer_re * cos_twist + outer_im * sin_twist
    turn_im = outer_im * cos_twist - outer_re * sin_twist
    spec_re = jnp.einsum("wckb,bf->wckf", turn_re, cos_inner, precision=high) + jnp.einsum(
        "wckb,bf->wckf", turn_im, sin_inner, precision=high
    )
    spec_im = jnp.einsum("wckb,bf->wckf", turn_im, cos_inner, precision=high) - jnp.einsum(
        "wckb,bf->wckf", turn_re, sin_inner, precision=high
    )
    prod_re = spec_re[0] * spec_re[1] - spec_im[0] * spec_im[1]
    prod_im = spec_re[0] * spec_im[1] + spec_im[0] * spec_re[1]
    inner_re = jnp.einsum("ckf,fb->ckb", prod_re, cos_inner, precision=high) - jnp.einsum(
        "ckf,fb->ckb", prod_im, sin_inner, precision=high
    )
    inner_im = jnp.einsum("ckf,fb->ckb", prod_im, cos_inner, precision=high) + jnp.einsum(
        "ckf,fb->ckb", prod_re, sin_inner, precision=high
    )
    back_re = inner_re * cos_twist - inner_im * sin_twist
    back_im = inner_im * cos_twist + inner_re * sin_twist
    cos_final, sin_final = tables(blocks_io, freq_io, 2 * groups)
    result = jnp.einsum("ak,ckb->cab", cos_final, back_re, precision=high) - jnp.einsum(
        "ak,ckb->cab", sin_final, back_im, precision=high
    )
    return (result / total).reshape(chans, groups * rows)


def shards(projected, short_weight, filter_taps, skip_gain, stream, norm_gain):
    rows = projected.shape[0]
    groups = lax.axis_size("seq")
    previous = shifted(projected[rows - 2 :], "seq", 1)
    ext = jnp.concatenate([previous, projected], axis=0).astype(jnp.float32)
    featured = short_weight[0] * ext[2:] + short_weight[1] * ext[1:-1] + short_weight[2] * ext[:-2]
    x_one = featured[:, 0]
    gated = featured[:, 1] * featured[:, 2]
    whole = lax.all_to_all(
        jnp.stack([gated, filter_taps]), "seq", split_axis=2, concat_axis=1, tiled=True
    )
    signals = jnp.transpose(whole, (0, 2, 1))
    convolved = local_convolve(signals, groups, rows)
    conv = lax.all_to_all(convolved.T, "seq", split_axis=0, concat_axis=1, tiled=True)
    mixer = (conv + skip_gain * gated) * x_one
    mixed = mixer.astype(jnp.bfloat16)
    summed = stream.astype(jnp.float32) + mixer
    power = lax.psum(jnp.sum(summed * summed, axis=1), "chan")
    normed = (summed / jnp.sqrt(power[:, None] / D + 1e-05) * norm_gain).astype(jnp.bfloat16)
    return (mixed, normed)


MESH = pl.DeviceIdType.MESH
POWER = 16
TOP = 2.0**7.75


def encode(x):
    most = jnp.maximum(jnp.max(jnp.abs(x), axis=0, keepdims=True), 1e-30)
    r = x * (TOP / most)
    p = r * r
    p = p * p
    p = p * p
    p = p * p
    return jnp.where(r < 0.0, -p, p).astype(jnp.bfloat16), most * (1.0 / TOP)


def decode(code, scale):
    y = code.astype(jnp.float32)
    mag = jnp.abs(y)
    root = jnp.exp(jnp.log(jnp.maximum(mag, 1e-38)) * (1.0 / POWER)) * scale
    root = jnp.where(mag > 0.0, root, 0.0)
    return jnp.where(y < 0.0, -root, root)


def split3(x):
    hi = x.astype(jnp.bfloat16)
    lo = (x - hi.astype(jnp.float32)).astype(jnp.bfloat16)
    return jnp.concatenate([hi, lo, hi], axis=0)


def dot(a, b):
    return jnp.dot(a, b, preferred_element_type=jnp.float32)


def wide(mat):
    hi = mat.astype(ml_dtypes.bfloat16)
    lo = (mat - hi.astype(np.float64)).astype(ml_dtypes.bfloat16)
    return np.concatenate([hi, hi, lo], axis=1)


def constants(groups, rows, fine):
    total = 2 * groups * rows
    ks = groups + 2
    k = np.arange(ks)
    a = np.arange(groups)
    b = np.arange(rows)
    live = (k <= groups).astype(np.float64)
    angle = 2.0 * np.pi * (k[:, None] * a[None, :] % (2 * groups)) / (2 * groups)
    eye = np.eye(fine)
    fwd = np.stack([np.cos(angle), -np.sin(angle)], axis=1) * live[:, None, None]
    outer = np.einsum("kra,xy->krxay", fwd, eye).reshape(ks * 2 * fine, groups * fine)
    weight = np.where((k == 0) | (k == groups), 1.0, 2.0) * live / total
    back = np.einsum("kra,xy->axkry", fwd * weight[:, None, None], eye)
    back = back.reshape(groups * fine, ks * 2 * fine)
    inner = 2.0 * np.pi * (b[:, None] * b[None, :] % rows) / rows
    c, s = np.cos(inner), np.sin(inner)
    mat = np.block([[c, s], [-s, c]])
    turn = 2.0 * np.pi * (k[:, None] * b[None, :] % total) / total
    spread = np.stack([np.cos(turn), np.sin(turn)], axis=1)[..., None]
    spread = np.broadcast_to(spread, (ks, 2, rows, 128)).astype(np.float32)
    return wide(outer), wide(mat), wide(mat.T), wide(back), spread


def outer_forward(n, begin, end, outer, x, y):
    ks = n + 2

    def step(j, carry):
        parts = []
        for half in range(2):
            at = pl.ds(pl.multiple_of(j * 32 + 16 * half, 16), 16)
            parts.append(x[:, at, :].reshape(n * 16, 128))
        u = dot(outer[...], split3(jnp.concatenate(parts, axis=1)))
        for half in range(2):
            at = pl.ds(pl.multiple_of(j * 32 + 16 * half, 16), 16)
            y[:, :, at, :] = u[:, 128 * half : 128 * half + 128].reshape(ks, 2, 16, 128)
        return carry

    lax.fori_loop(begin // 32, end // 32, step, 0)


def inner_forward(pair, rows, inner, turn, y):
    parts = []
    for half in range(2):
        k = 2 * pair + half
        re, im, c, s = y[k, 0], y[k, 1], turn[k, 0], turn[k, 1]
        parts.append(jnp.concatenate([re * c + im * s, im * c - re * s], axis=0))
    return dot(inner[...], split3(jnp.concatenate(parts, axis=1)))


def kernel(
    n, x_hbm, w_hbm, taps_hbm, skip_hbm, stream_hbm, gain_hbm, outer_hbm, inner_hbm, inner_back_hbm,
    back_hbm, turn_hbm, mixed_ref, normed_ref,
    x_ref, w_ref, taps_ref, skip_ref, stream_ref, gain_ref, outer, inner, inner_back, back, turn,
    gated_ref, one_ref, tail, halo, hsend, hsscale, hcode, hscale, gsend, gsscale, gcode, gscale,
    csend, csscale, ccode, cscale, x, y, z, summed, mine, other, sems, edge_sems, local_sems,
):
    me = lax.axis_index("seq")
    core = lax.axis_index("chan")
    rows = x_ref.shape[1]
    half_rows = rows // 2
    spans = ((0, rows // 4), (rows // 4, rows))
    barrier = pltpu.get_barrier_semaphore()

    def greet(o, carry):
        pl.semaphore_signal(
            barrier, inc=1, device_id={"seq": lax.rem(me + o, n)}, device_id_type=MESH
        )
        return carry

    lax.fori_loop(1, n, greet, 0)
    pl.semaphore_signal(barrier, inc=1, device_id={"chan": 1 - core}, device_id_type=MESH)

    moves = [(x_hbm, x_ref), (taps_hbm, taps_ref), (w_hbm, w_ref), (outer_hbm, outer),
             (turn_hbm, turn), (inner_hbm, inner), (inner_back_hbm, inner_back), (back_hbm, back),
             (stream_hbm, stream_ref), (skip_hbm, skip_ref), (gain_hbm, gain_ref)]
    loads = []
    for i, (src, dst) in enumerate(moves):
        load = pltpu.make_async_copy(src, dst, local_sems.at[i])
        load.start()
        loads.append(load)

    def lanes(d):
        return pl.ds(pl.multiple_of(d * 128, 128), 128)

    def link(kind, o, src, dst):
        return pltpu.make_async_remote_copy(
            src_ref=src,
            dst_ref=dst,
            send_sem=sems.at[2 * kind, o],
            recv_sem=sems.at[2 * kind + 1, o],
            device_id={"seq": lax.rem(me + o, n)},
            device_id_type=MESH,
        )

    def taps_links(o):
        to = lax.rem(me + o, n)
        return (link(0, o, hsend.at[to], hcode.at[me]), link(1, o, hsscale.at[to], hscale.at[me]))

    def gated_links(o):
        to = lax.rem(me + o, n)
        low, high = pl.ds(0, half_rows), pl.ds(half_rows, half_rows)
        return (
            link(2, o, gsend.at[to, low], gcode.at[me, low]),
            link(3, o, gsscale.at[to], gscale.at[me]),
            link(4, o, gsend.at[to, high], gcode.at[me, high]),
        )

    def conv_links(p, o):
        to = lax.rem(me + o, n)
        at = pl.ds(spans[p][0], spans[p][1] - spans[p][0])
        return (
            link(5 + 2 * p, o, csend.at[to, at], ccode.at[me, at]),
            link(6 + 2 * p, o, csscale.at[p, to], cscale.at[p, me]),
        )

    loads[1].wait()

    def pack_taps(o, carry):
        to = lax.rem(me + o, n)
        hsend[to], hsscale[to] = encode(taps_ref[:, lanes(to)])
        return carry

    lax.fori_loop(1, n, pack_taps, 0)
    loads[0].wait()
    for j in range(3):
        last = x_ref[j, rows - 16 :, :].astype(jnp.float32)
        tail[2 * j : 2 * j + 2, :] = last[14:16, :]
    pl.semaphore_wait(barrier, n)
    after = pltpu.make_async_remote_copy(
        src_ref=tail,
        dst_ref=halo,
        send_sem=edge_sems.at[0],
        recv_sem=edge_sems.at[1],
        device_id={"seq": lax.rem(me + 1, n)},
        device_id_type=MESH,
    )
    after.start()

    def send_taps(o, carry):
        for copy in taps_links(o):
            copy.start()
        return carry

    lax.fori_loop(1, n, send_taps, 0)
    x[me] = taps_ref[:, lanes(me)]
    loads[2].wait()
    after.wait()
    first = jnp.where(me > 0, 1.0, 0.0).astype(jnp.float32)

    def feature(d):
        cols = lanes(d)
        prev = halo[:, cols] * first
        feats = []
        for j in range(3):
            now = x_ref[j, :, cols].astype(jnp.float32)
            ext = jnp.concatenate([prev[2 * j : 2 * j + 2], now], axis=0)
            feats.append(
                w_ref[0, j : j + 1, cols] * now
                + w_ref[1, j : j + 1, cols] * ext[1 : rows + 1]
                + w_ref[2, j : j + 1, cols] * ext[:rows]
            )
        gated = feats[1] * feats[2]
        one_ref[:, cols] = feats[0]
        gated_ref[:, cols] = gated
        return gated

    def send_gated(o, carry):
        to = lax.rem(me + o, n)
        gsend[to], gsscale[to] = encode(feature(to))
        for copy in gated_links(o)[:2]:
            copy.start()
        return carry

    lax.fori_loop(1, n, send_gated, 0)

    def send_rest(o, carry):
        gated_links(o)[2].start()
        return carry

    lax.fori_loop(1, n, send_rest, 0)
    feature(me)

    def take_taps(o, carry):
        source = lax.rem(me - o + n, n)
        for copy in taps_links(o):
            copy.wait()
        x[source] = decode(hcode[source], hscale[source])
        return carry

    lax.fori_loop(1, n, take_taps, 0)
    for load in loads[3:8]:
        load.wait()
    outer_forward(n, 0, rows, outer, x, y)

    def spectrum(pair, carry):
        z[pair] = inner_forward(pair, rows, inner, turn, y)
        return carry

    lax.fori_loop(0, (n + 2) // 2, spectrum, 0)
    x[me] = gated_ref[:, lanes(me)]

    def take_low(o, carry):
        source = lax.rem(me - o + n, n)
        for copy in gated_links(o)[:2]:
            copy.wait()
        x[source, :half_rows, :] = decode(gcode[source, :half_rows, :], gscale[source])
        return carry

    def take_high(o, carry):
        source = lax.rem(me - o + n, n)
        gated_links(o)[2].wait()
        x[source, half_rows:, :] = decode(gcode[source, half_rows:, :], gscale[source])
        return carry

    lax.fori_loop(1, n, take_low, 0)
    outer_forward(n, 0, half_rows, outer, x, y)
    lax.fori_loop(1, n, take_high, 0)
    outer_forward(n, half_rows, rows, outer, x, y)

    def multiply(pair, carry):
        g = inner_forward(pair, rows, inner, turn, y)
        h = z[pair]
        gr, gi, hr, hi = g[:rows], g[rows:], h[:rows], h[rows:]
        prod = jnp.concatenate([gr * hr - gi * hi, gr * hi + gi * hr], axis=0)
        v = dot(inner_back[...], split3(prod))
        for half in range(2):
            k = 2 * pair + half
            side = slice(128 * half, 128 * half + 128)
            re, im, c, s = v[:rows, side], v[rows:, side], turn[k, 0], turn[k, 1]
            y[k, 0] = re * c - im * s
            y[k, 1] = im * c + re * s
        return carry

    lax.fori_loop(0, (n + 2) // 2, multiply, 0)

    def blocks(j, carry):
        parts = []
        for half in range(2):
            at = pl.ds(pl.multiple_of(j * 32 + 16 * half, 16), 16)
            parts.append(y[:, :, at, :].reshape((n + 2) * 32, 128))
        u = dot(back[...], split3(jnp.concatenate(parts, axis=1)))
        for half in range(2):
            at = pl.ds(pl.multiple_of(j * 32 + 16 * half, 16), 16)
            x[:, at, :] = u[:, 128 * half : 128 * half + 128].reshape(n, 16, 128)
        return carry

    for p in range(2):
        lax.fori_loop(spans[p][0] // 32, spans[p][1] // 32, blocks, 0)

        def send_conv(o, carry, p=p):
            to = lax.rem(me + o, n)
            at = pl.ds(spans[p][0], spans[p][1] - spans[p][0])
            csend[to, at, :], csscale[p, to] = encode(x[to, at, :])
            for copy in conv_links(p, o):
                copy.start()
            return carry

        lax.fori_loop(1, n, send_conv, 0)

    for load in loads[8:]:
        load.wait()
    mine[...] = jnp.zeros_like(mine)

    def mix(at, d, conv):
        cols = lanes(d)
        mixer = (conv + skip_ref[:, cols] * gated_ref[at, cols]) * one_ref[at, cols]
        mixed_ref[at, cols] = mixer.astype(jnp.bfloat16)
        both = stream_ref[at, cols].astype(jnp.float32) + mixer
        summed[at, cols] = both
        mine[at, :] += both * both

    swaps = []
    for p in range(2):
        at = pl.ds(spans[p][0], spans[p][1] - spans[p][0])
        mix(at, me, x[me, at, :])

        def take_conv(o, carry, p=p, at=at):
            source = lax.rem(me - o + n, n)
            for copy in conv_links(p, o):
                copy.wait()
            mix(at, source, decode(ccode[source, at, :], cscale[p, source]))
            return carry

        lax.fori_loop(1, n, take_conv, 0)
        swap = pltpu.make_async_remote_copy(
            src_ref=mine.at[at],
            dst_ref=other.at[at],
            send_sem=edge_sems.at[2 + 2 * p],
            recv_sem=edge_sems.at[3 + 2 * p],
            device_id={"chan": 1 - core},
            device_id_type=MESH,
        )
        swap.start()
        swaps.append(swap)

    for p in range(2):
        at = pl.ds(spans[p][0], spans[p][1] - spans[p][0])
        swaps[p].wait()
        power = jnp.sum(mine[at, :] + other[at, :], axis=1, keepdims=True)
        factor = 1.0 / jnp.sqrt(power / D + 1e-05)

        def norm(d, carry, at=at, factor=factor):
            cols = lanes(d)
            normed = summed[at, cols] * factor * gain_ref[:, cols]
            normed_ref[at, cols] = normed.astype(jnp.bfloat16)
            return carry

        lax.fori_loop(0, n, norm, 0)


def fast(n, projected, short_weight, filter_taps, skip_gain, stream, norm_gain):
    rows, _, chans = projected.shape
    f32, bf16 = jnp.float32, jnp.bfloat16
    codes, scales, ks = (n, rows, 128), (n, 1, 128), n + 2
    operands = [
        jnp.transpose(projected, (1, 0, 2)), short_weight, filter_taps,
        skip_gain.reshape(1, chans), stream, norm_gain.reshape(1, chans),
    ] + [jnp.asarray(table) for table in constants(n, rows, 16)]
    pair = [pltpu.VMEM(codes, bf16), pltpu.VMEM(scales, f32)]
    return pl.pallas_call(
        functools.partial(kernel, n),
        out_shape=[jax.ShapeDtypeStruct((rows, chans), bf16)] * 2,
        in_specs=[pl.BlockSpec(memory_space=pl.ANY)] * len(operands),
        out_specs=[pl.BlockSpec(memory_space=pltpu.VMEM)] * 2,
        scratch_shapes=[pltpu.VMEM(array.shape, array.dtype) for array in operands]
        + [pltpu.VMEM((rows, chans), f32)] * 2
        + [pltpu.VMEM((8, chans), f32)] * 2
        + pair * 4
        + [pltpu.VMEM(codes, bf16), pltpu.VMEM((2,) + scales, f32)] * 2
        + [
            pltpu.VMEM(codes, f32),
            pltpu.VMEM((ks, 2, rows, 128), f32),
            pltpu.VMEM((ks // 2, 2 * rows, 256), f32),
            pltpu.VMEM((rows, chans), f32),
            pltpu.VMEM((rows, 128), f32),
            pltpu.VMEM((rows, 128), f32),
            pltpu.SemaphoreType.DMA((18, n)),
            pltpu.SemaphoreType.DMA((6,)),
            pltpu.SemaphoreType.DMA((len(operands),)),
        ],
        compiler_params=pltpu.CompilerParams(
            collective_id=0, has_side_effects=True, vmem_limit_bytes=56 * 2**20
        ),
        name="mixer",
    )(*operands)


def solution(mesh):
    n, cores = mesh.shape["seq"], mesh.shape["chan"]

    def local(*args):
        rows, _, chans = args[0].shape
        if cores == 2 and chans == 128 * n and rows == 128 and n % 2 == 0:
            return tuple(fast(n, *args))
        return shards(*args)

    in_specs = (
        P("seq", None, "chan"),
        P(None, None, "chan"),
        P("seq", "chan"),
        P("chan"),
        P("seq", "chan"),
        P("chan"),
    )
    out_specs = (P("seq", "chan"), P("seq", "chan"))
    return jax.shard_map(local, mesh=mesh, in_specs=in_specs, out_specs=out_specs, check_vma=False)
```

```python
import functools
import math

import jax
import jax.numpy as jnp
import ml_dtypes
import numpy as np
from jax import lax
from jax.experimental import pallas as pl
from jax.experimental.pallas import tpu as pltpu
from jax.sharding import PartitionSpec as P

D = 4096


high = lax.Precision.HIGHEST


def shifted(x, axis, by):
    count = lax.axis_size(axis)
    pairs = [(i, i + by) for i in range(count) if 0 <= i + by < count]
    return lax.ppermute(x, axis, pairs)


def tables(rows, cols, length):
    product = rows[:, None] * cols[None, :] % length
    angle = 2.0 * math.pi / length * product.astype(jnp.float32)
    return (jnp.cos(angle), jnp.sin(angle))


def local_convolve(signals, groups, rows):
    total = 2 * groups * rows
    chans = signals.shape[1]
    blocks_io = jnp.arange(groups, dtype=jnp.int32)
    freq_io = jnp.arange(2 * groups, dtype=jnp.int32)
    pos_io = jnp.arange(rows, dtype=jnp.int32)
    cos_outer, sin_outer = tables(freq_io, blocks_io, 2 * groups)
    cos_twist, sin_twist = tables(freq_io, pos_io, total)
    cos_inner, sin_inner = tables(pos_io, pos_io, rows)
    shaped = signals.reshape(2, chans, groups, rows)
    outer_re = jnp.einsum("ka,wcab->wckb", cos_outer, shaped, precision=high)
    outer_im = -jnp.einsum("ka,wcab->wckb", sin_outer, shaped, precision=high)
    turn_re = outer_re * cos_twist + outer_im * sin_twist
    turn_im = outer_im * cos_twist - outer_re * sin_twist
    spec_re = jnp.einsum("wckb,bf->wckf", turn_re, cos_inner, precision=high) + jnp.einsum(
        "wckb,bf->wckf", turn_im, sin_inner, precision=high
    )
    spec_im = jnp.einsum("wckb,bf->wckf", turn_im, cos_inner, precision=high) - jnp.einsum(
        "wckb,bf->wckf", turn_re, sin_inner, precision=high
    )
    prod_re = spec_re[0] * spec_re[1] - spec_im[0] * spec_im[1]
    prod_im = spec_re[0] * spec_im[1] + spec_im[0] * spec_re[1]
    inner_re = jnp.einsum("ckf,fb->ckb", prod_re, cos_inner, precision=high) - jnp.einsum(
        "ckf,fb->ckb", prod_im, sin_inner, precision=high
    )
    inner_im = jnp.einsum("ckf,fb->ckb", prod_im, cos_inner, precision=high) + jnp.einsum(
        "ckf,fb->ckb", prod_re, sin_inner, precision=high
    )
    back_re = inner_re * cos_twist - inner_im * sin_twist
    back_im = inner_im * cos_twist + inner_re * sin_twist
    cos_final, sin_final = tables(blocks_io, freq_io, 2 * groups)
    result = jnp.einsum("ak,ckb->cab", cos_final, back_re, precision=high) - jnp.einsum(
        "ak,ckb->cab", sin_final, back_im, precision=high
    )
    return (result / total).reshape(chans, groups * rows)


def shards(projected, short_weight, filter_taps, skip_gain, stream, norm_gain):
    rows = projected.shape[0]
    groups = lax.axis_size("seq")
    previous = shifted(projected[rows - 2 :], "seq", 1)
    ext = jnp.concatenate([previous, projected], axis=0).astype(jnp.float32)
    featured = short_weight[0] * ext[2:] + short_weight[1] * ext[1:-1] + short_weight[2] * ext[:-2]
    x_one = featured[:, 0]
    gated = featured[:, 1] * featured[:, 2]
    whole = lax.all_to_all(
        jnp.stack([gated, filter_taps]), "seq", split_axis=2, concat_axis=1, tiled=True
    )
    signals = jnp.transpose(whole, (0, 2, 1))
    convolved = local_convolve(signals, groups, rows)
    conv = lax.all_to_all(convolved.T, "seq", split_axis=0, concat_axis=1, tiled=True)
    mixer = (conv + skip_gain * gated) * x_one
    mixed = mixer.astype(jnp.bfloat16)
    summed = stream.astype(jnp.float32) + mixer
    power = lax.psum(jnp.sum(summed * summed, axis=1), "chan")
    normed = (summed / jnp.sqrt(power[:, None] / D + 1e-05) * norm_gain).astype(jnp.bfloat16)
    return (mixed, normed)


MESH = pl.DeviceIdType.MESH
POWER = 16
TOP = 2.0**7.75


def encode(x):
    most = jnp.maximum(jnp.max(jnp.abs(x), axis=0, keepdims=True), 1e-30)
    r = x * (TOP / most)
    p = r * r
    p = p * p
    p = p * p
    p = p * p
    return jnp.where(r < 0.0, -p, p).astype(jnp.bfloat16), most * (1.0 / TOP)


def decode(code, scale):
    y = code.astype(jnp.float32)
    mag = jnp.abs(y)
    root = jnp.exp(jnp.log(jnp.maximum(mag, 1e-38)) * (1.0 / POWER)) * scale
    root = jnp.where(mag > 0.0, root, 0.0)
    return jnp.where(y < 0.0, -root, root)


def split3(x):
    hi = x.astype(jnp.bfloat16)
    lo = (x - hi.astype(jnp.float32)).astype(jnp.bfloat16)
    return jnp.concatenate([hi, lo, hi], axis=0)


def dot(a, b):
    return jnp.dot(a, b, preferred_element_type=jnp.float32)


def wide(mat):
    hi = mat.astype(ml_dtypes.bfloat16)
    lo = (mat - hi.astype(np.float64)).astype(ml_dtypes.bfloat16)
    return np.concatenate([hi, hi, lo], axis=1)


def constants(groups, rows, fine):
    total = 2 * groups * rows
    ks = groups + 2
    k = np.arange(ks)
    a = np.arange(groups)
    b = np.arange(rows)
    live = (k <= groups).astype(np.float64)
    angle = 2.0 * np.pi * (k[:, None] * a[None, :] % (2 * groups)) / (2 * groups)
    eye = np.eye(fine)
    fwd = np.stack([np.cos(angle), -np.sin(angle)], axis=1) * live[:, None, None]
    outer = np.einsum("kra,xy->krxay", fwd, eye).reshape(ks * 2 * fine, groups * fine)
    weight = np.where((k == 0) | (k == groups), 1.0, 2.0) * live / total
    back = np.einsum("kra,xy->axkry", fwd * weight[:, None, None], eye)
    back = back.reshape(groups * fine, ks * 2 * fine)
    inner = 2.0 * np.pi * (b[:, None] * b[None, :] % rows) / rows
    c, s = np.cos(inner), np.sin(inner)
    mat = np.block([[c, s], [-s, c]])
    turn = 2.0 * np.pi * (k[:, None] * b[None, :] % total) / total
    spread = np.stack([np.cos(turn), np.sin(turn)], axis=1)[..., None]
    spread = np.broadcast_to(spread, (ks, 2, rows, 128)).astype(np.float32)
    return wide(outer), wide(mat), wide(mat.T), wide(back), spread


def outer_forward(n, begin, end, outer, x, y):
    ks = n + 2

    def step(j, carry):
        parts = []
        for half in range(2):
            at = pl.ds(pl.multiple_of(j * 32 + 16 * half, 16), 16)
            parts.append(x[:, at, :].reshape(n * 16, 128))
        u = dot(outer[...], split3(jnp.concatenate(parts, axis=1)))
        for half in range(2):
            at = pl.ds(pl.multiple_of(j * 32 + 16 * half, 16), 16)
            y[:, :, at, :] = u[:, 128 * half : 128 * half + 128].reshape(ks, 2, 16, 128)
        return carry

    lax.fori_loop(begin // 32, end // 32, step, 0, unroll=True)


def inner_forward(pair, rows, inner, turn, y):
    parts = []
    for half in range(2):
        k = 2 * pair + half
        re, im, c, s = y[k, 0], y[k, 1], turn[k, 0], turn[k, 1]
        parts.append(jnp.concatenate([re * c + im * s, im * c - re * s], axis=0))
    return dot(inner[...], split3(jnp.concatenate(parts, axis=1)))


def kernel(
    n, x_hbm, w_hbm, taps_hbm, skip_hbm, stream_hbm, gain_hbm, outer_hbm, inner_hbm, inner_back_hbm,
    back_hbm, turn_hbm, mixed_ref, normed_ref,
    x_ref, w_ref, taps_ref, skip_ref, stream_ref, gain_ref, outer, inner, inner_back, back, turn,
    gated_ref, one_ref, tail, halo, hsend, hsscale, hcode, hscale, gsend, gsscale, gcode, gscale,
    csend, csscale, ccode, cscale, x, y, z, summed, mine, other, sems, edge_sems, local_sems,
):
    me = lax.axis_index("seq")
    core = lax.axis_index("chan")
    rows = x_ref.shape[1]
    half_rows = rows // 2
    spans = ((0, rows // 4), (rows // 4, rows))
    barrier = pltpu.get_barrier_semaphore()

    def greet(o, carry):
        pl.semaphore_signal(
            barrier, inc=1, device_id={"seq": lax.rem(me + o, n)}, device_id_type=MESH
        )
        return carry

    lax.fori_loop(1, n, greet, 0)
    pl.semaphore_signal(barrier, inc=1, device_id={"chan": 1 - core}, device_id_type=MESH)

    moves = [(x_hbm, x_ref), (taps_hbm, taps_ref), (w_hbm, w_ref), (outer_hbm, outer),
             (turn_hbm, turn), (inner_hbm, inner), (inner_back_hbm, inner_back), (back_hbm, back),
             (stream_hbm, stream_ref), (skip_hbm, skip_ref), (gain_hbm, gain_ref)]
    loads = []
    for i, (src, dst) in enumerate(moves):
        load = pltpu.make_async_copy(src, dst, local_sems.at[i])
        load.start()
        loads.append(load)

    def lanes(d):
        return pl.ds(pl.multiple_of(d * 128, 128), 128)

    def link(kind, o, src, dst):
        return pltpu.make_async_remote_copy(
            src_ref=src,
            dst_ref=dst,
            send_sem=sems.at[2 * kind, o],
            recv_sem=sems.at[2 * kind + 1, o],
            device_id={"seq": lax.rem(me + o, n)},
            device_id_type=MESH,
        )

    def taps_links(o):
        to = lax.rem(me + o, n)
        return (link(0, o, hsend.at[to], hcode.at[me]), link(1, o, hsscale.at[to], hscale.at[me]))

    def gated_links(o):
        to = lax.rem(me + o, n)
        low, high = pl.ds(0, half_rows), pl.ds(half_rows, half_rows)
        return (
            link(2, o, gsend.at[to, low], gcode.at[me, low]),
            link(3, o, gsscale.at[to], gscale.at[me]),
            link(4, o, gsend.at[to, high], gcode.at[me, high]),
        )

    def conv_links(p, o):
        to = lax.rem(me + o, n)
        at = pl.ds(spans[p][0], spans[p][1] - spans[p][0])
        return (
            link(5 + 2 * p, o, csend.at[to, at], ccode.at[me, at]),
            link(6 + 2 * p, o, csscale.at[p, to], cscale.at[p, me]),
        )

    loads[1].wait()

    def pack_taps(o, carry):
        to = lax.rem(me + o, n)
        hsend[to], hsscale[to] = encode(taps_ref[:, lanes(to)])
        return carry

    lax.fori_loop(1, n, pack_taps, 0)
    loads[0].wait()
    for j in range(3):
        last = x_ref[j, rows - 16 :, :].astype(jnp.float32)
        tail[2 * j : 2 * j + 2, :] = last[14:16, :]
    pl.semaphore_wait(barrier, n)
    after = pltpu.make_async_remote_copy(
        src_ref=tail,
        dst_ref=halo,
        send_sem=edge_sems.at[0],
        recv_sem=edge_sems.at[1],
        device_id={"seq": lax.rem(me + 1, n)},
        device_id_type=MESH,
    )
    after.start()

    def send_taps(o, carry):
        for copy in taps_links(o):
            copy.start()
        return carry

    lax.fori_loop(1, n, send_taps, 0)
    x[me] = taps_ref[:, lanes(me)]
    loads[2].wait()
    after.wait()
    first = jnp.where(me > 0, 1.0, 0.0).astype(jnp.float32)

    def feature(d):
        cols = lanes(d)
        prev = halo[:, cols] * first
        feats = []
        for j in range(3):
            now = x_ref[j, :, cols].astype(jnp.float32)
            ext = jnp.concatenate([prev[2 * j : 2 * j + 2], now], axis=0)
            feats.append(
                w_ref[0, j : j + 1, cols] * now
                + w_ref[1, j : j + 1, cols] * ext[1 : rows + 1]
                + w_ref[2, j : j + 1, cols] * ext[:rows]
            )
        gated = feats[1] * feats[2]
        one_ref[:, cols] = feats[0]
        gated_ref[:, cols] = gated
        return gated

    def send_gated(o, carry):
        to = lax.rem(me + o, n)
        gsend[to], gsscale[to] = encode(feature(to))
        for copy in gated_links(o)[:2]:
            copy.start()
        return carry

    lax.fori_loop(1, n, send_gated, 0)

    def send_rest(o, carry):
        gated_links(o)[2].start()
        return carry

    lax.fori_loop(1, n, send_rest, 0)
    feature(me)

    def take_taps(o, carry):
        source = lax.rem(me - o + n, n)
        for copy in taps_links(o):
            copy.wait()
        x[source] = decode(hcode[source], hscale[source])
        return carry

    lax.fori_loop(1, n, take_taps, 0)
    for load in loads[3:8]:
        load.wait()
    outer_forward(n, 0, rows, outer, x, y)

    def spectrum(pair, carry):
        z[pair] = inner_forward(pair, rows, inner, turn, y)
        return carry

    lax.fori_loop(0, (n + 2) // 2, spectrum, 0)
    x[me] = gated_ref[:, lanes(me)]

    def take_low(o, carry):
        source = lax.rem(me - o + n, n)
        for copy in gated_links(o)[:2]:
            copy.wait()
        x[source, :half_rows, :] = decode(gcode[source, :half_rows, :], gscale[source])
        return carry

    def take_high(o, carry):
        source = lax.rem(me - o + n, n)
        gated_links(o)[2].wait()
        x[source, half_rows:, :] = decode(gcode[source, half_rows:, :], gscale[source])
        return carry

    lax.fori_loop(1, n, take_low, 0)
    outer_forward(n, 0, half_rows, outer, x, y)
    lax.fori_loop(1, n, take_high, 0)
    outer_forward(n, half_rows, rows, outer, x, y)

    def multiply(pair, carry):
        g = inner_forward(pair, rows, inner, turn, y)
        h = z[pair]
        gr, gi, hr, hi = g[:rows], g[rows:], h[:rows], h[rows:]
        prod = jnp.concatenate([gr * hr - gi * hi, gr * hi + gi * hr], axis=0)
        v = dot(inner_back[...], split3(prod))
        for half in range(2):
            k = 2 * pair + half
            side = slice(128 * half, 128 * half + 128)
            re, im, c, s = v[:rows, side], v[rows:, side], turn[k, 0], turn[k, 1]
            y[k, 0] = re * c - im * s
            y[k, 1] = im * c + re * s
        return carry

    lax.fori_loop(0, (n + 2) // 2, multiply, 0, unroll=True)

    def blocks(j, carry):
        parts = []
        for half in range(2):
            at = pl.ds(pl.multiple_of(j * 32 + 16 * half, 16), 16)
            parts.append(y[:, :, at, :].reshape((n + 2) * 32, 128))
        u = dot(back[...], split3(jnp.concatenate(parts, axis=1)))
        for half in range(2):
            at = pl.ds(pl.multiple_of(j * 32 + 16 * half, 16), 16)
            x[:, at, :] = u[:, 128 * half : 128 * half + 128].reshape(n, 16, 128)
        return carry

    for p in range(2):
        lax.fori_loop(spans[p][0] // 32, spans[p][1] // 32, blocks, 0, unroll=True)

        def send_conv(o, carry, p=p):
            to = lax.rem(me + o, n)
            at = pl.ds(spans[p][0], spans[p][1] - spans[p][0])
            csend[to, at, :], csscale[p, to] = encode(x[to, at, :])
            for copy in conv_links(p, o):
                copy.start()
            return carry

        lax.fori_loop(1, n, send_conv, 0)

    for load in loads[8:]:
        load.wait()
    mine[...] = jnp.zeros_like(mine)

    def mix(at, d, conv):
        cols = lanes(d)
        mixer = (conv + skip_ref[:, cols] * gated_ref[at, cols]) * one_ref[at, cols]
        mixed_ref[at, cols] = mixer.astype(jnp.bfloat16)
        both = stream_ref[at, cols].astype(jnp.float32) + mixer
        summed[at, cols] = both
        mine[at, :] += both * both

    swaps = []
    for p in range(2):
        at = pl.ds(spans[p][0], spans[p][1] - spans[p][0])
        mix(at, me, x[me, at, :])

        def take_conv(o, carry, p=p, at=at):
            source = lax.rem(me - o + n, n)
            for copy in conv_links(p, o):
                copy.wait()
            mix(at, source, decode(ccode[source, at, :], cscale[p, source]))
            return carry

        lax.fori_loop(1, n, take_conv, 0)
        swap = pltpu.make_async_remote_copy(
            src_ref=mine.at[at],
            dst_ref=other.at[at],
            send_sem=edge_sems.at[2 + 2 * p],
            recv_sem=edge_sems.at[3 + 2 * p],
            device_id={"chan": 1 - core},
            device_id_type=MESH,
        )
        swap.start()
        swaps.append(swap)

    for p in range(2):
        at = pl.ds(spans[p][0], spans[p][1] - spans[p][0])
        swaps[p].wait()
        power = jnp.sum(mine[at, :] + other[at, :], axis=1, keepdims=True)
        factor = 1.0 / jnp.sqrt(power / D + 1e-05)

        def norm(d, carry, at=at, factor=factor):
            cols = lanes(d)
            normed = summed[at, cols] * factor * gain_ref[:, cols]
            normed_ref[at, cols] = normed.astype(jnp.bfloat16)
            return carry

        lax.fori_loop(0, n, norm, 0)


def fast(n, projected, short_weight, filter_taps, skip_gain, stream, norm_gain):
    rows, _, chans = projected.shape
    f32, bf16 = jnp.float32, jnp.bfloat16
    codes, scales, ks = (n, rows, 128), (n, 1, 128), n + 2
    operands = [
        jnp.transpose(projected, (1, 0, 2)), short_weight, filter_taps,
        skip_gain.reshape(1, chans), stream, norm_gain.reshape(1, chans),
    ] + [jnp.asarray(table) for table in constants(n, rows, 16)]
    pair = [pltpu.VMEM(codes, bf16), pltpu.VMEM(scales, f32)]
    return pl.pallas_call(
        functools.partial(kernel, n),
        out_shape=[jax.ShapeDtypeStruct((rows, chans), bf16)] * 2,
        in_specs=[pl.BlockSpec(memory_space=pl.ANY)] * len(operands),
        out_specs=[pl.BlockSpec(memory_space=pltpu.VMEM)] * 2,
        scratch_shapes=[pltpu.VMEM(array.shape, array.dtype) for array in operands]
        + [pltpu.VMEM((rows, chans), f32)] * 2
        + [pltpu.VMEM((8, chans), f32)] * 2
        + pair * 4
        + [pltpu.VMEM(codes, bf16), pltpu.VMEM((2,) + scales, f32)] * 2
        + [
            pltpu.VMEM(codes, f32),
            pltpu.VMEM((ks, 2, rows, 128), f32),
            pltpu.VMEM((ks // 2, 2 * rows, 256), f32),
            pltpu.VMEM((rows, chans), f32),
            pltpu.VMEM((rows, 128), f32),
            pltpu.VMEM((rows, 128), f32),
            pltpu.SemaphoreType.DMA((18, n)),
            pltpu.SemaphoreType.DMA((6,)),
            pltpu.SemaphoreType.DMA((len(operands),)),
        ],
        compiler_params=pltpu.CompilerParams(
            collective_id=0, has_side_effects=True, vmem_limit_bytes=56 * 2**20
        ),
        name="mixer",
    )(*operands)


def solution(mesh):
    n, cores = mesh.shape["seq"], mesh.shape["chan"]

    def local(*args):
        rows, _, chans = args[0].shape
        if cores == 2 and chans == 128 * n and rows == 128 and n % 2 == 0:
            return tuple(fast(n, *args))
        return shards(*args)

    in_specs = (
        P("seq", None, "chan"),
        P(None, None, "chan"),
        P("seq", "chan"),
        P("chan"),
        P("seq", "chan"),
        P("chan"),
    )
    out_specs = (P("seq", "chan"), P("seq", "chan"))
    return jax.shard_map(local, mesh=mesh, in_specs=in_specs, out_specs=out_specs, check_vma=False)
```
